32 devices in a mesh: grp: 2 (over x), tok: 16 (over z, y, core).
Axes of the slice: x: 2, y: 2, z: 4, core: 2. Of those that a mesh axis runs over, the one named last changes fastest.
Arguments:
- tokens: bfloat16 [4096, 2048], P(('grp', 'tok')), parts along dimension 0, may hold values from -6 to 6
- norm_gain: float32 [2048], replicated, may hold values from 0.1 to 1.9
- expert_ids: int32 [4096, 8], P(('grp', 'tok')), parts along dimension 0, may hold values from 0 to 15, as said below
- gate_weights: float32 [4096, 8], P(('grp', 'tok')), parts along dimension 0, may hold values from 0.05 to 1
- owner_map: int32 [16], replicated, may hold values from 0 to 15, each once
- in_q: bfloat16 [16, 2, 2048, 768], P('tok'), may hold values from -0.125 to 0.125
- in_scale: bfloat16 [16, 2, 768], P('tok'), may hold values from 0.5 to 2
- down_q: bfloat16 [16, 768, 2048], P('tok'), may hold values from -0.21875 to 0.21875
- down_scale: bfloat16 [16, 2048], P('tok'), may hold values from 0.5 to 2
Outputs:
- moe_out: bfloat16 [4096, 2048], P(('grp', 'tok')), parts along dimension 0
The draws below stay inside these ranges and needn't reach their ends.
There are 2 independent parts, one for each index of `grp`. The reference program is written for one: setup_inputs(seed, part) draws one part's arguments, and reference() takes and returns one part's arrays. A program takes and returns all parts, laid end to end along the dimension named above; an argument that names none is the same for every part. Nothing has to cross between parts.
Inputs may be any that keep to these rules, and one draw needn't show every extreme that they name: `expert_ids`: each row names 8 different experts. One and the same expert is named by exactly 96 of the 128 rows of every device; every other expert is named by between 32 and 80 rows of each device, and 80 is reached on every device. `owner_map`: every slot holds exactly one expert.
All inputs are finite; a program needn't handle non-finite values.
Results may differ from the reference program's by a relative error of at most 0.0071.
Values may be sent and summed in bfloat16 or wider, within the bound.
A program may use at most 128 MiB of HBM per device.

```python
import math
import jax
import jax.numpy as jnp
from jax import lax

D = 2048
FF = 768
TOP = 8
TOK_DEV = 128
EXPERTS = 16
TOKENS = 2048
MOST = 96
N_TOK = 16


def block_routes(block_key, hot_expert):
    mean_load = TOK_DEV * TOP // EXPERTS
    spread = mean_load // 4
    pair_count = (EXPERTS - 2) // 2
    key_order, key_amount, key_rows, key_columns = jax.random.split(block_key, 4)
    labels = jnp.arange(EXPERTS, dtype=jnp.int32)
    shuffled = jax.random.permutation(key_order, EXPERTS).astype(jnp.int32)
    ranking = jnp.where(labels == hot_expert, -1, shuffled)
    expert_order = jnp.argsort(ranking).astype(jnp.int32)
    amounts = jax.random.randint(key_amount, (pair_count,), 0, spread + 1).astype(jnp.int32)
    amounts = amounts.at[0].set(spread)
    head = jnp.full((1,), mean_load + mean_load // 2, jnp.int32)
    tail = jnp.full((1,), mean_load - mean_load // 2, jnp.int32)
    load_counts = jnp.concatenate([head, mean_load + amounts, mean_load - amounts, tail])
    load_ends = jnp.cumsum(load_counts).astype(jnp.int32)
    position = jnp.arange(TOK_DEV * TOP, dtype=jnp.int32)
    group_index = jnp.searchsorted(load_ends, position, side='right').astype(jnp.int32)
    listed = expert_order[group_index]
    table_grid = listed.reshape(TOP, TOK_DEV).T
    table_grid = table_grid[jax.random.permutation(key_rows, TOK_DEV)]
    column_noise = jax.random.randint(key_columns, (TOK_DEV, TOP), 0, 1 << 20).astype(jnp.int32) * TOP
    column_noise = column_noise + jnp.arange(TOP, dtype=jnp.int32)
    column_order = jnp.argsort(column_noise, axis=1)
    return jnp.take_along_axis(table_grid, column_order, axis=1)


def draw_expert_ids(key, part):
    base_key = jax.random.fold_in(key, 17)
    key_hot, key_blocks = jax.random.split(base_key)
    hot_expert = jax.random.randint(key_hot, (), 0, EXPERTS).astype(jnp.int32)
    block_keys = jax.random.split(key_blocks, TOKENS // TOK_DEV)
    routes = jax.vmap(block_routes, in_axes=(0, None))(block_keys, hot_expert)
    return routes.reshape(TOKENS, TOP).astype(jnp.int32)


def levels(key, shape, shards, low, top_value):
    def one(dim, parts):
        heights = jax.random.uniform(jax.random.fold_in(jax.random.fold_in(key, 6), dim), (parts,), jnp.float32, low / len(shards), top_value / len(shards))
        return jnp.repeat(jnp.exp(heights), shape[dim] // parts).reshape((-1,) + (1,) * (len(shape) - dim - 1))

    level = one(*shards[0])
    for cut in shards[1:]:
        level = level * one(*cut)
    return level


def centred(key, shape, width, reach, cuts=(), held_as=jnp.bfloat16):
    factor_of = levels(key, shape, cuts, -0.22, 0.18) if cuts else 1.0
    values = jax.random.normal(key, shape, jnp.float32) * width * factor_of
    return jnp.minimum(jnp.maximum(values, -reach), reach).astype(held_as)


def setup_inputs(seed: int = 0, part: int = 0) -> dict:
    arg_keys = jax.random.split(jax.random.key(seed), 10)
    part_keys = jax.random.split(jax.random.fold_in(arg_keys[9], part), 10)
    tokens = centred(part_keys[0], (TOKENS, D), 1.0, 6.0, ((0, 16),))
    norm_gain = jnp.clip(1.0 + 0.18 * jax.random.normal(arg_keys[1], (D,), jnp.float32), 0.1, 1.9)
    expert_ids = draw_expert_ids(jax.random.fold_in(jax.random.fold_in(arg_keys[9], part), 71), part)
    gate_weights = jnp.clip(jnp.exp(math.log(1.0) - 2.9957323 * jax.random.uniform(part_keys[3], (TOKENS, TOP), jnp.float32) ** levels(part_keys[3], (TOKENS, TOP), ((0, 16),), -0.2, 0.2)), 0.05, 1.0)
    owner_map = jax.random.permutation(arg_keys[4], EXPERTS).astype(jnp.int32)
    in_q = centred(arg_keys[5], (EXPERTS, 2, D, FF), D ** -0.5, 0.125, ((0, 16),))
    in_scale = jnp.clip(jnp.exp(math.log(2.0) - 1.3862944 * jax.random.uniform(arg_keys[6], (EXPERTS, 2, FF), jnp.float32) ** levels(arg_keys[6], (EXPERTS, 2, FF), ((0, 16),), -0.2, 0.2)), 0.5, 2.0).astype(jnp.bfloat16)
    down_q = centred(arg_keys[7], (EXPERTS, FF, D), FF ** -0.5, 0.21875, ((0, 16),))
    down_scale = jnp.clip(jnp.exp(math.log(2.0) - 1.3862944 * jax.random.uniform(arg_keys[8], (EXPERTS, D), jnp.float32) ** levels(arg_keys[8], (EXPERTS, D), ((0, 16),), -0.2, 0.2)), 0.5, 2.0).astype(jnp.bfloat16)
    return dict(tokens=tokens, norm_gain=norm_gain, expert_ids=expert_ids, gate_weights=gate_weights, owner_map=owner_map, in_q=in_q, in_scale=in_scale, down_q=down_q, down_scale=down_scale)


def expert_rows(batch_rows, in_blocks, in_scales, down_block, down_scales):
    gate_part = jnp.dot(batch_rows, in_blocks[0], preferred_element_type=jnp.float32) * in_scales[0]
    up_part = jnp.dot(batch_rows, in_blocks[1], preferred_element_type=jnp.float32) * in_scales[1]
    hidden = (jax.nn.silu(gate_part) * up_part).astype(jnp.bfloat16)
    return (jnp.dot(hidden, down_block, preferred_element_type=jnp.float32) * down_scales).astype(jnp.bfloat16)

def reference(tokens, norm_gain, expert_ids, gate_weights, owner_map, in_q, in_scale, down_q, down_scale):
    values = tokens.astype(jnp.float32)
    row_scale = lax.rsqrt(lax.optimization_barrier(jnp.mean(values * values, axis=1, keepdims=True)) + 1e-06)
    normed = (values * row_scale * norm_gain).astype(jnp.bfloat16)
    weights = gate_weights / lax.optimization_barrier(jnp.sum(gate_weights, axis=1, keepdims=True))
    flat_slot = owner_map[expert_ids].reshape(-1).astype(jnp.int32)
    flat_weight = weights.reshape(-1)
    assigned = TOKENS * TOP
    limit = N_TOK * MOST
    padded_rows = jnp.concatenate([normed, jnp.zeros((1, D), jnp.bfloat16)], axis=0)
    padded_weight = jnp.concatenate([flat_weight, jnp.zeros((1,), jnp.float32)], axis=0)

    def visit(total, pack):
        slot_id, in_blocks, in_scales, down_block, down_scales = pack
        chosen = jnp.nonzero(flat_slot == slot_id, size=limit, fill_value=assigned)[0].astype(jnp.int32)
        token_index = (chosen // TOP).astype(jnp.int32)
        served = expert_rows(padded_rows[token_index], in_blocks, in_scales, down_block, down_scales)
        share = padded_weight[chosen][:, None] * served.astype(jnp.float32)
        return (total.at[token_index].add(share), None)
    start_total = jnp.zeros((TOKENS + 1, D), jnp.float32)
    slot_ids = jnp.arange(EXPERTS, dtype=jnp.int32)
    total, unused = lax.scan(visit, start_total, (slot_ids, in_q, in_scale, down_q, down_scale))
    return total[:TOKENS].astype(jnp.bfloat16)
```

```python
import jax
import jax.numpy as jnp
from jax import lax
from jax.sharding import PartitionSpec as P


def expert_rows(batch_rows, in_blocks, in_scales, down_block, down_scales):
    gate_part = jnp.dot(batch_rows, in_blocks[0], preferred_element_type=jnp.float32) * in_scales[0]
    up_part = jnp.dot(batch_rows, in_blocks[1], preferred_element_type=jnp.float32) * in_scales[1]
    hidden = (jax.nn.silu(gate_part) * up_part).astype(jnp.bfloat16)
    return (jnp.dot(hidden, down_block, preferred_element_type=jnp.float32) * down_scales).astype(
        jnp.bfloat16
    )


def normalised(tokens, norm_gain):
    values = tokens.astype(jnp.float32)
    row_scale = lax.rsqrt(jnp.mean(values * values, axis=1, keepdims=True) + 1e-06)
    return (values * row_scale * norm_gain).astype(jnp.bfloat16)


def dispatched(
    tokens, norm_gain, expert_ids, gate_weights, owner_map, in_q, in_scale, down_q, down_scale
):
    tok_rows, model_width = tokens.shape
    top_count = expert_ids.shape[1]
    experts = owner_map.shape[0]
    mean_load = tok_rows * top_count // experts
    capacity = mean_load + mean_load // 2
    normed = normalised(tokens, norm_gain)
    weights = gate_weights / jnp.sum(gate_weights, axis=1, keepdims=True)
    labels = jnp.arange(experts, dtype=jnp.int32)
    slot_table = jnp.sum(jnp.where(expert_ids[:, :, None] == labels, owner_map, 0), axis=2)
    flat_slot = slot_table.reshape(-1)
    onehot = (flat_slot[:, None] == labels).astype(jnp.bfloat16)
    count = flat_slot.shape[0]
    before = jnp.tri(count, count, -1, dtype=jnp.bfloat16)
    ranks = jnp.dot(before, onehot, preferred_element_type=jnp.float32)
    slot_rank = jnp.sum(ranks * onehot, axis=1).astype(jnp.int32)
    repeated = jnp.repeat(normed, top_count, axis=0)
    outgoing = (
        jnp.zeros((experts, capacity, model_width), jnp.bfloat16)
        .at[flat_slot, slot_rank]
        .set(repeated)
    )
    received = lax.all_to_all(outgoing, "tok", split_axis=0, concat_axis=0, tiled=True)
    source_count, slot_count, unused_width = received.shape
    flat_rows = received.reshape(source_count * slot_count, model_width)
    served = expert_rows(flat_rows, in_q[0], in_scale[0], down_q[0], down_scale[0])
    served = served.reshape(source_count, slot_count, model_width)
    returned_rows = lax.all_to_all(served, "tok", split_axis=0, concat_axis=0, tiled=True)
    picked = returned_rows[flat_slot, slot_rank].reshape(tok_rows, top_count, model_width)
    mixed = jnp.sum(weights[:, :, None] * picked.astype(jnp.float32), axis=1)
    return mixed.astype(jnp.bfloat16)


def gathered(
    tokens, norm_gain, expert_ids, gate_weights, owner_map, in_q, in_scale, down_q, down_scale
):
    me = lax.axis_index("tok")
    experts = owner_map.shape[0]
    normed = normalised(tokens, norm_gain)
    weights = gate_weights / jnp.sum(gate_weights, axis=1, keepdims=True)
    labels = jnp.arange(experts, dtype=jnp.int32)
    slot_table = jnp.sum(jnp.where(expert_ids[:, :, None] == labels, owner_map, 0), axis=2)
    shares = jnp.sum(jnp.where(slot_table[:, :, None] == labels, weights[:, :, None], 0.0), axis=1)
    all_rows = lax.all_gather(normed, "tok", axis=0, tiled=True)
    all_shares = lax.all_gather(shares, "tok", axis=0, tiled=True)
    share = jnp.sum(jnp.where(labels == me, all_shares, 0.0), axis=1, keepdims=True)
    gate_part = jnp.dot(all_rows, in_q[0, 0], preferred_element_type=jnp.float32) * in_scale[0, 0]
    up_part = jnp.dot(all_rows, in_q[0, 1], preferred_element_type=jnp.float32) * in_scale[0, 1]
    hidden = (jax.nn.silu(gate_part) * up_part).astype(jnp.bfloat16)
    served = jnp.dot(hidden, down_q[0], preferred_element_type=jnp.float32) * down_scale[0]
    part = (served * share).astype(jnp.bfloat16)
    return lax.psum_scatter(part, "tok", scatter_dimension=0, tiled=True)


def solution(mesh):
    in_specs = (
        P(("grp", "tok"), None),
        P(),
        P(("grp", "tok"), None),
        P(("grp", "tok"), None),
        P(),
        P("tok", None, None, None),
        P("tok", None, None),
        P("tok", None, None),
        P("tok", None),
    )
    out_specs = P(("grp", "tok"), None)

    def on_device(*args):
        experts, top_count = args[4].shape[0], args[2].shape[1]
        body = gathered if experts <= 2 * top_count else dispatched
        return body(*args)

    return jax.shard_map(
        on_device, mesh=mesh, in_specs=in_specs, out_specs=out_specs, check_vma=False
    )
```

```python
import functools

import jax
import jax.numpy as jnp
from jax import lax
from jax.experimental import pallas as pl
from jax.experimental.pallas import tpu as pltpu
from jax.sharding import PartitionSpec as P


def expert_rows(batch_rows, in_blocks, in_scales, down_block, down_scales):
    gate_part = jnp.dot(batch_rows, in_blocks[0], preferred_element_type=jnp.float32) * in_scales[0]
    up_part = jnp.dot(batch_rows, in_blocks[1], preferred_element_type=jnp.float32) * in_scales[1]
    hidden = (jax.nn.silu(gate_part) * up_part).astype(jnp.bfloat16)
    return (jnp.dot(hidden, down_block, preferred_element_type=jnp.float32) * down_scales).astype(
        jnp.bfloat16
    )


def normalised(tokens, norm_gain):
    values = tokens.astype(jnp.float32)
    row_scale = lax.rsqrt(jnp.mean(values * values, axis=1, keepdims=True) + 1e-06)
    return (values * row_scale * norm_gain).astype(jnp.bfloat16)


def dispatched(
    tokens, norm_gain, expert_ids, gate_weights, owner_map, in_q, in_scale, down_q, down_scale
):
    tok_rows, model_width = tokens.shape
    top_count = expert_ids.shape[1]
    experts = owner_map.shape[0]
    mean_load = tok_rows * top_count // experts
    capacity = mean_load + mean_load // 2
    normed = normalised(tokens, norm_gain)
    weights = gate_weights / jnp.sum(gate_weights, axis=1, keepdims=True)
    labels = jnp.arange(experts, dtype=jnp.int32)
    slot_table = jnp.sum(jnp.where(expert_ids[:, :, None] == labels, owner_map, 0), axis=2)
    flat_slot = slot_table.reshape(-1)
    onehot = (flat_slot[:, None] == labels).astype(jnp.bfloat16)
    count = flat_slot.shape[0]
    before = jnp.tri(count, count, -1, dtype=jnp.bfloat16)
    ranks = jnp.dot(before, onehot, preferred_element_type=jnp.float32)
    slot_rank = jnp.sum(ranks * onehot, axis=1).astype(jnp.int32)
    repeated = jnp.repeat(normed, top_count, axis=0)
    outgoing = (
        jnp.zeros((experts, capacity, model_width), jnp.bfloat16)
        .at[flat_slot, slot_rank]
        .set(repeated)
    )
    received = lax.all_to_all(outgoing, "tok", split_axis=0, concat_axis=0, tiled=True)
    source_count, slot_count, unused_width = received.shape
    flat_rows = received.reshape(source_count * slot_count, model_width)
    served = expert_rows(flat_rows, in_q[0], in_scale[0], down_q[0], down_scale[0])
    served = served.reshape(source_count, slot_count, model_width)
    returned_rows = lax.all_to_all(served, "tok", split_axis=0, concat_axis=0, tiled=True)
    picked = returned_rows[flat_slot, slot_rank].reshape(tok_rows, top_count, model_width)
    mixed = jnp.sum(weights[:, :, None] * picked.astype(jnp.float32), axis=1)
    return mixed.astype(jnp.bfloat16)


def ring_kernel(
    chips, experts, x_ref, in_ref, in_scale_ref, down_ref, down_scale_ref, out_ref,
    rows, part, sib_in, ring_out, ring_in,
    right_send, right_recv, left_send, left_recv, sib_send, sib_recv,
    give_send, give_recv, sum_send, sum_recv,
):
    depth = chips // 2
    model = out_ref.shape[1]
    half = model // 2
    me = lax.axis_index("tok")
    core = lax.rem(me, 2)
    chip = me // 2
    place = chip // 2 + lax.rem(chip, 2) * (2 * depth - 1 - 2 * (chip // 2))

    def chip_at(position):
        position = lax.rem(position + 2 * chips, chips)
        back = position // depth
        return 2 * (position + back * (2 * depth - 1 - 2 * position)) + back

    right = 2 * chip_at(place + 1) + core
    left = 2 * chip_at(place - 1) + core
    sibling = 2 * chip + 1 - core

    def remote(src, dst, send, recv, target):
        return pltpu.make_async_remote_copy(
            src_ref=src, dst_ref=dst, send_sem=send, recv_sem=recv,
            device_id={"tok": target}, device_id_type=pl.DeviceIdType.MESH,
        )

    def row_copy(position, side, send, recv, target):
        block = rows.at[chip_at(position), side]
        return remote(block, block, send, recv, target)

    def go_right(k, position):
        return row_copy(position, core, right_send.at[k], right_recv.at[k], right)

    def go_left(k, position):
        return row_copy(position, core, left_send.at[k], left_recv.at[k], left)

    def share(offset, side):
        return row_copy(place + offset, side, sib_send.at[offset], sib_recv.at[offset], sibling)

    def give(offset):
        block = chip_at(place + offset)
        return remote(
            part.at[block, 1 - core], sib_in.at[block], give_send.at[offset], give_recv.at[offset], sibling
        )

    rows[chip, core] = x_ref[...]
    barrier = pltpu.get_barrier_semaphore()
    for target in (left, right, sibling):
        pl.semaphore_signal(
            barrier, inc=1, device_id={"tok": target}, device_id_type=pl.DeviceIdType.MESH
        )
    pl.semaphore_wait(barrier, 3)

    far_right, far_left = chips // 2, chips - 1 - chips // 2
    go_right(0, place).start()
    go_left(0, place).start()
    share(0, core).start()

    def gather_step(k, carry):
        back = lax.rem(chips - k, chips)

        @pl.when(k >= 1)
        def _():
            go_right(k - 1, place - k).wait_recv()

            @pl.when(k < far_right)
            def _():
                go_right(k, place - k).start()

            share(back, core).start()

        @pl.when((k >= 1) & (k <= far_left))
        def _():
            go_left(k - 1, place + k).wait_recv()

            @pl.when(k < far_left)
            def _():
                go_left(k, place + k).start()

            share(k, core).start()

        sides = jnp.where((k >= 1) & (k <= far_left), 2, 1)

        def serve(turn, inner):
            offset = jnp.where(turn == 0, back, k)
            share(offset, 1 - core).wait_recv()
            block = chip_at(place + offset)
            batch = rows[block].reshape(-1, rows.shape[3])
            lanes = batch[:, model:].astype(jnp.float32)
            lane = lax.broadcasted_iota(jnp.int32, lanes.shape, 1)
            chosen = (lane == me) | (lane == me + experts) | (lane == me + 2 * experts)
            weight = jnp.sum(jnp.where(chosen, lanes, 0.0), axis=1, keepdims=True)
            values = batch[:, :model]
            gate = jnp.dot(values, in_ref[0], preferred_element_type=jnp.float32)
            gate = gate * in_scale_ref[0:1, :].astype(jnp.float32)
            up = jnp.dot(values, in_ref[1], preferred_element_type=jnp.float32)
            up = up * in_scale_ref[1:2, :].astype(jnp.float32)
            hidden = (gate / (1.0 + jnp.exp(-gate)) * up).astype(jnp.bfloat16)
            wide = model // 4
            for piece in range(4):
                cut = slice(piece * wide, (piece + 1) * wide)
                served = jnp.dot(hidden, down_ref[:, cut], preferred_element_type=jnp.float32)
                served = served * down_scale_ref[:, cut].astype(jnp.float32) * weight
                part[block, :, :, cut] = served.astype(jnp.bfloat16).reshape(2, -1, wide)
            give(offset).start()
            return inner

        return lax.fori_loop(0, sides, serve, carry)

    lax.fori_loop(0, far_right + 1, gather_step, 0)

    def sum_copy(way, step):
        target = right if way == 0 else left
        return remote(
            ring_out.at[way, step], ring_in.at[way, step],
            sum_send.at[way, step], sum_recv.at[way, step], target,
        )

    def own(offset, way):
        block = chip_at(place + offset)
        cut = slice(way * half, (way + 1) * half)
        return part[block, core, :, cut].astype(jnp.float32) + sib_in[block, :, cut].astype(jnp.float32)

    def take(offset, carry):
        give(offset).wait()
        return carry

    lax.fori_loop(0, chips, take, 0)
    for way, first in ((0, chips - 1), (1, 1)):
        ring_out[way, 0] = own(first, way).astype(jnp.bfloat16)
        sum_copy(way, 0).start()

    def sum_step(step, carry):
        for way in range(2):
            offset = chips - 1 - step if way == 0 else 1 + step
            mine = own(offset, way)
            sum_copy(way, step - 1).wait_recv()
            ring_out[way, step] = (mine + ring_in[way, step - 1].astype(jnp.float32)).astype(jnp.bfloat16)
            sum_copy(way, step).start()
        return carry

    lax.fori_loop(1, chips - 1, sum_step, 0)
    for way in range(2):
        mine = own(0, way)
        sum_copy(way, chips - 2).wait_recv()
        total = mine + ring_in[way, chips - 2].astype(jnp.float32)
        out_ref[:, way * half : (way + 1) * half] = total.astype(jnp.bfloat16)

    def ended(step, carry):
        sum_copy(0, step).wait_send()
        sum_copy(1, step).wait_send()
        return carry

    lax.fori_loop(0, chips - 1, ended, 0)

    def shared(offset, carry):
        share(offset, core).wait_send()
        return carry

    lax.fori_loop(0, chips, shared, 0)
    for k in range(far_right):
        go_right(k, place - k).wait_send()
    for k in range(far_left):
        go_left(k, place + k).wait_send()


def gathered(
    tokens, norm_gain, expert_ids, gate_weights, owner_map, in_q, in_scale, down_q, down_scale
):
    experts = owner_map.shape[0]
    tok_rows, model = tokens.shape
    chips = experts // 2
    normed = normalised(tokens, norm_gain)
    weights = gate_weights / jnp.sum(gate_weights, axis=1, keepdims=True)
    labels = jnp.arange(experts, dtype=jnp.int32)
    slot_table = jnp.sum(jnp.where(expert_ids[:, :, None] == labels, owner_map, 0), axis=2)
    shares = jnp.sum(jnp.where(slot_table[:, :, None] == labels, weights[:, :, None], 0.0), axis=1)
    high = lax.reduce_precision(shares, 8, 7)
    middle = lax.reduce_precision(shares - high, 8, 7)
    low = shares - high - middle
    lanes = jnp.concatenate([high, middle, low], axis=1).astype(jnp.bfloat16)
    pad = -lanes.shape[1] % 128
    rows = jnp.concatenate([normed, jnp.pad(lanes, ((0, 0), (0, pad)))], axis=1)
    width = rows.shape[1]
    vmem = pl.BlockSpec(memory_space=pltpu.VMEM)
    dma = pltpu.SemaphoreType.DMA
    total_rows = 2 * chips * tok_rows
    half = model // 2
    return pl.pallas_call(
        functools.partial(ring_kernel, chips, experts),
        out_shape=jax.ShapeDtypeStruct((tok_rows, model), jnp.bfloat16),
        in_specs=[vmem] * 5,
        out_specs=vmem,
        scratch_shapes=[
            pltpu.VMEM((chips, 2, tok_rows, width), jnp.bfloat16),
            pltpu.VMEM((chips, 2, tok_rows, model), jnp.bfloat16),
            pltpu.VMEM((chips, tok_rows, model), jnp.bfloat16),
            pltpu.VMEM((2, chips - 1, tok_rows, half), jnp.bfloat16),
            pltpu.VMEM((2, chips - 1, tok_rows, half), jnp.bfloat16),
            dma((chips,)), dma((chips,)), dma((chips,)), dma((chips,)), dma((chips,)), dma((chips,)),
            dma((chips,)), dma((chips,)), dma((2, chips - 1)), dma((2, chips - 1)),
        ],
        compiler_params=pltpu.CompilerParams(
            collective_id=0, has_side_effects=True, vmem_limit_bytes=60 * 1024 * 1024
        ),
        cost_estimate=pl.CostEstimate(
            flops=6 * total_rows * model * in_q.shape[3], bytes_accessed=4 * total_rows * model, transcendentals=0
        ),
    )(rows, in_q[0], in_scale[0], down_q[0], down_scale)


def solution(mesh):
    in_specs = (
        P(("grp", "tok"), None),
        P(),
        P(("grp", "tok"), None),
        P(("grp", "tok"), None),
        P(),
        P("tok", None, None, None),
        P("tok", None, None),
        P("tok", None, None),
        P("tok", None),
    )
    out_specs = P(("grp", "tok"), None)

    def on_device(*args):
        experts, top_count = args[4].shape[0], args[2].shape[1]
        body = gathered if experts <= 2 * top_count and experts % 4 == 0 else dispatched
        return body(*args)

    return jax.shard_map(
        on_device, mesh=mesh, in_specs=in_specs, out_specs=out_specs, check_vma=False
    )
```

```python
import functools

import jax
import jax.numpy as jnp
from jax import lax
from jax.experimental import pallas as pl
from jax.experimental.pallas import tpu as pltpu
from jax.sharding import PartitionSpec as P


def expert_rows(batch_rows, in_blocks, in_scales, down_block, down_scales):
    gate_part = jnp.dot(batch_rows, in_blocks[0], preferred_element_type=jnp.float32) * in_scales[0]
    up_part = jnp.dot(batch_rows, in_blocks[1], preferred_element_type=jnp.float32) * in_scales[1]
    hidden = (jax.nn.silu(gate_part) * up_part).astype(jnp.bfloat16)
    return (jnp.dot(hidden, down_block, preferred_element_type=jnp.float32) * down_scales).astype(
        jnp.bfloat16
    )


def normalised(tokens, norm_gain):
    values = tokens.astype(jnp.float32)
    row_scale = lax.rsqrt(jnp.mean(values * values, axis=1, keepdims=True) + 1e-06)
    return (values * row_scale * norm_gain).astype(jnp.bfloat16)


def dispatched(
    tokens, norm_gain, expert_ids, gate_weights, owner_map, in_q, in_scale, down_q, down_scale
):
    tok_rows, model_width = tokens.shape
    top_count = expert_ids.shape[1]
    experts = owner_map.shape[0]
    mean_load = tok_rows * top_count // experts
    capacity = mean_load + mean_load // 2
    normed = normalised(tokens, norm_gain)
    weights = gate_weights / jnp.sum(gate_weights, axis=1, keepdims=True)
    labels = jnp.arange(experts, dtype=jnp.int32)
    slot_table = jnp.sum(jnp.where(expert_ids[:, :, None] == labels, owner_map, 0), axis=2)
    flat_slot = slot_table.reshape(-1)
    onehot = (flat_slot[:, None] == labels).astype(jnp.bfloat16)
    count = flat_slot.shape[0]
    before = jnp.tri(count, count, -1, dtype=jnp.bfloat16)
    ranks = jnp.dot(before, onehot, preferred_element_type=jnp.float32)
    slot_rank = jnp.sum(ranks * onehot, axis=1).astype(jnp.int32)
    repeated = jnp.repeat(normed, top_count, axis=0)
    outgoing = (
        jnp.zeros((experts, capacity, model_width), jnp.bfloat16)
        .at[flat_slot, slot_rank]
        .set(repeated)
    )
    received = lax.all_to_all(outgoing, "tok", split_axis=0, concat_axis=0, tiled=True)
    source_count, slot_count, unused_width = received.shape
    flat_rows = received.reshape(source_count * slot_count, model_width)
    served = expert_rows(flat_rows, in_q[0], in_scale[0], down_q[0], down_scale[0])
    served = served.reshape(source_count, slot_count, model_width)
    returned_rows = lax.all_to_all(served, "tok", split_axis=0, concat_axis=0, tiled=True)
    picked = returned_rows[flat_slot, slot_rank].reshape(tok_rows, top_count, model_width)
    mixed = jnp.sum(weights[:, :, None] * picked.astype(jnp.float32), axis=1)
    return mixed.astype(jnp.bfloat16)


def ring_kernel(
    chips, experts, x_ref, in_hbm, in_scale_ref, down_hbm, down_scale_ref, out_ref,
    in_ref, down_ref, load_sem, rows, part, sib_in, ring_out, ring_in,
    right_send, right_recv, left_send, left_recv, sib_send, sib_recv,
    give_send, give_recv, sum_send, sum_recv,
):
    depth = chips // 2
    model = out_ref.shape[1]
    half = model // 2
    me = lax.axis_index("tok")
    core = lax.rem(me, 2)
    chip = me // 2
    place = chip // 2 + lax.rem(chip, 2) * (2 * depth - 1 - 2 * (chip // 2))

    def chip_at(position):
        position = lax.rem(position + 2 * chips, chips)
        back = position // depth
        return 2 * (position + back * (2 * depth - 1 - 2 * position)) + back

    right = 2 * chip_at(place + 1) + core
    left = 2 * chip_at(place - 1) + core
    sibling = 2 * chip + 1 - core

    def remote(src, dst, send, recv, target):
        return pltpu.make_async_remote_copy(
            src_ref=src, dst_ref=dst, send_sem=send, recv_sem=recv,
            device_id={"tok": target}, device_id_type=pl.DeviceIdType.MESH,
        )

    def row_copy(position, side, send, recv, target):
        block = rows.at[chip_at(position), side]
        return remote(block, block, send, recv, target)

    def go_right(k, position):
        return row_copy(position, core, right_send.at[k], right_recv.at[k], right)

    def go_left(k, position):
        return row_copy(position, core, left_send.at[k], left_recv.at[k], left)

    def share(offset, side):
        return row_copy(place + offset, side, sib_send.at[offset], sib_recv.at[offset], sibling)

    def give(offset):
        block = chip_at(place + offset)
        return remote(
            part.at[block, 1 - core], sib_in.at[block], give_send.at[offset], give_recv.at[offset], sibling
        )

    loads = (
        pltpu.make_async_copy(in_hbm, in_ref, load_sem.at[0]),
        pltpu.make_async_copy(down_hbm, down_ref, load_sem.at[1]),
    )
    for load in loads:
        load.start()
    rows[chip, core] = x_ref[...]
    barrier = pltpu.get_barrier_semaphore()
    for target in (left, right, sibling):
        pl.semaphore_signal(
            barrier, inc=1, device_id={"tok": target}, device_id_type=pl.DeviceIdType.MESH
        )
    pl.semaphore_wait(barrier, 3)

    far_right, far_left = chips // 2, chips - 1 - chips // 2
    go_right(0, place).start()
    go_left(0, place).start()
    share(0, core).start()
    for load in loads:
        load.wait()

    def sum_copy(way, step):
        target = right if way == 0 else left
        return remote(
            ring_out.at[way, step], ring_in.at[way, step],
            sum_send.at[way, step], sum_recv.at[way, step], target,
        )

    def own(offset, way):
        block = chip_at(place + offset)
        cut = slice(way * half, (way + 1) * half)
        return part[block, core, :, cut].astype(jnp.float32) + sib_in[block, :, cut].astype(jnp.float32)

    def sum_step(step, carry):
        for way in range(2):
            offset = chips - 1 - step if way == 0 else 1 + step
            @pl.when((step < far_left) | ((step == far_left) & (way == 0)))
            def _():
                give(offset).wait()

            mine = own(offset, way)
            sum_copy(way, step - 1).wait_recv()
            ring_out[way, step] = (mine + ring_in[way, step - 1].astype(jnp.float32)).astype(jnp.bfloat16)
            sum_copy(way, step).start()
        return carry

    def gather_step(k, carry):
        back = lax.rem(chips - k, chips)

        @pl.when(k >= 1)
        def _():
            go_right(k - 1, place - k).wait_recv()

            @pl.when(k < far_right)
            def _():
                go_right(k, place - k).start()

            share(back, core).start()

        @pl.when((k >= 1) & (k <= far_left))
        def _():
            go_left(k - 1, place + k).wait_recv()

            @pl.when(k < far_left)
            def _():
                go_left(k, place + k).start()

            share(k, core).start()

        sides = jnp.where((k >= 1) & (k <= far_left), 2, 1)

        def serve(turn, inner):
            offset = jnp.where(turn == 0, back, k)
            share(offset, 1 - core).wait_recv()
            block = chip_at(place + offset)
            batch = rows[block].reshape(-1, rows.shape[3])
            lanes = batch[:, model:].astype(jnp.float32)
            lane = lax.broadcasted_iota(jnp.int32, lanes.shape, 1)
            chosen = (lane == me) | (lane == me + experts) | (lane == me + 2 * experts)
            weight = jnp.sum(jnp.where(chosen, lanes, 0.0), axis=1, keepdims=True)
            values = batch[:, :model]
            gate = jnp.dot(values, in_ref[0], preferred_element_type=jnp.float32)
            gate = gate * in_scale_ref[0:1, :].astype(jnp.float32)
            up = jnp.dot(values, in_ref[1], preferred_element_type=jnp.float32)
            up = up * in_scale_ref[1:2, :].astype(jnp.float32)
            hidden = (gate / (1.0 + jnp.exp(-gate)) * up).astype(jnp.bfloat16)
            wide = model // 4
            for piece in range(4):
                cut = slice(piece * wide, (piece + 1) * wide)
                served = jnp.dot(hidden, down_ref[:, cut], preferred_element_type=jnp.float32)
                served = served * down_scale_ref[:, cut].astype(jnp.float32) * weight
                part[block, :, :, cut] = served.astype(jnp.bfloat16).reshape(2, -1, wide)
            give(offset).start()
            return inner

        lax.fori_loop(0, sides, serve, 0)

        @pl.when(k == 1)
        def _():
            for way, first in ((0, chips - 1), (1, 1)):
                give(first).wait()
                ring_out[way, 0] = own(first, way).astype(jnp.bfloat16)
                sum_copy(way, 0).start()

        @pl.when(k >= 2)
        def _():
            sum_step(k - 1, 0)

        return carry

    lax.fori_loop(0, far_right + 1, gather_step, 0)

    lax.fori_loop(far_right, chips - 1, sum_step, 0)
    give(0).wait()
    for way in range(2):
        mine = own(0, way)
        sum_copy(way, chips - 2).wait_recv()
        total = mine + ring_in[way, chips - 2].astype(jnp.float32)
        out_ref[:, way * half : (way + 1) * half] = total.astype(jnp.bfloat16)

    def ended(step, carry):
        sum_copy(0, step).wait_send()
        sum_copy(1, step).wait_send()
        return carry

    lax.fori_loop(0, chips - 1, ended, 0)

    def shared(offset, carry):
        share(offset, core).wait_send()
        return carry

    lax.fori_loop(0, chips, shared, 0)
    for k in range(far_right):
        go_right(k, place - k).wait_send()
    for k in range(far_left):
        go_left(k, place + k).wait_send()


def gathered(
    tokens, norm_gain, expert_ids, gate_weights, owner_map, in_q, in_scale, down_q, down_scale
):
    experts = owner_map.shape[0]
    tok_rows, model = tokens.shape
    chips = experts // 2
    normed = normalised(tokens, norm_gain)
    weights = gate_weights / jnp.sum(gate_weights, axis=1, keepdims=True)
    labels = jnp.arange(experts, dtype=jnp.int32)
    slot_table = jnp.sum(jnp.where(expert_ids[:, :, None] == labels, owner_map, 0), axis=2)
    shares = jnp.sum(jnp.where(slot_table[:, :, None] == labels, weights[:, :, None], 0.0), axis=1)
    high = lax.reduce_precision(shares, 8, 7)
    middle = lax.reduce_precision(shares - high, 8, 7)
    low = shares - high - middle
    lanes = jnp.concatenate([high, middle, low], axis=1).astype(jnp.bfloat16)
    pad = -lanes.shape[1] % 128
    rows = jnp.concatenate([normed, jnp.pad(lanes, ((0, 0), (0, pad)))], axis=1)
    width = rows.shape[1]
    vmem = pl.BlockSpec(memory_space=pltpu.VMEM)
    dma = pltpu.SemaphoreType.DMA
    total_rows = 2 * chips * tok_rows
    half = model // 2
    return pl.pallas_call(
        functools.partial(ring_kernel, chips, experts),
        out_shape=jax.ShapeDtypeStruct((tok_rows, model), jnp.bfloat16),
        in_specs=[vmem, pl.BlockSpec(memory_space=pl.ANY), vmem, pl.BlockSpec(memory_space=pl.ANY), vmem],
        out_specs=vmem,
        scratch_shapes=[
            pltpu.VMEM(in_q.shape[1:], in_q.dtype),
            pltpu.VMEM(down_q.shape[1:], down_q.dtype),
            dma((2,)),
            pltpu.VMEM((chips, 2, tok_rows, width), jnp.bfloat16),
            pltpu.VMEM((chips, 2, tok_rows, model), jnp.bfloat16),
            pltpu.VMEM((chips, tok_rows, model), jnp.bfloat16),
            pltpu.VMEM((2, chips - 1, tok_rows, half), jnp.bfloat16),
            pltpu.VMEM((2, chips - 1, tok_rows, half), jnp.bfloat16),
            dma((chips,)), dma((chips,)), dma((chips,)), dma((chips,)), dma((chips,)), dma((chips,)),
            dma((chips,)), dma((chips,)), dma((2, chips - 1)), dma((2, chips - 1)),
        ],
        compiler_params=pltpu.CompilerParams(
            collective_id=0, has_side_effects=True, vmem_limit_bytes=60 * 1024 * 1024
        ),
        cost_estimate=pl.CostEstimate(
            flops=6 * total_rows * model * in_q.shape[3], bytes_accessed=4 * total_rows * model, transcendentals=0
        ),
    )(rows, in_q[0], in_scale[0], down_q[0], down_scale)


def solution(mesh):
    in_specs = (
        P(("grp", "tok"), None),
        P(),
        P(("grp", "tok"), None),
        P(("grp", "tok"), None),
        P(),
        P("tok", None, None, None),
        P("tok", None, None),
        P("tok", None, None),
        P("tok", None),
    )
    out_specs = P(("grp", "tok"), None)

    def on_device(*args):
        experts, top_count = args[4].shape[0], args[2].shape[1]
        body = gathered if experts <= 2 * top_count and experts % 4 == 0 else dispatched
        return body(*args)

    return jax.shard_map(
        on_device, mesh=mesh, in_specs=in_specs, out_specs=out_specs, check_vma=False
    )
```

```python
import functools

import jax
import jax.numpy as jnp
from jax import lax
from jax.experimental import pallas as pl
from jax.experimental.pallas import tpu as pltpu
from jax.sharding import PartitionSpec as P


def expert_rows(batch_rows, in_blocks, in_scales, down_block, down_scales):
    gate_part = jnp.dot(batch_rows, in_blocks[0], preferred_element_type=jnp.float32) * in_scales[0]
    up_part = jnp.dot(batch_rows, in_blocks[1], preferred_element_type=jnp.float32) * in_scales[1]
    hidden = (jax.nn.silu(gate_part) * up_part).astype(jnp.bfloat16)
    return (jnp.dot(hidden, down_block, preferred_element_type=jnp.float32) * down_scales).astype(
        jnp.bfloat16
    )


def normalised(tokens, norm_gain):
    values = tokens.astype(jnp.float32)
    row_scale = lax.rsqrt(jnp.mean(values * values, axis=1, keepdims=True) + 1e-06)
    return (values * row_scale * norm_gain).astype(jnp.bfloat16)


def dispatched(
    tokens, norm_gain, expert_ids, gate_weights, owner_map, in_q, in_scale, down_q, down_scale
):
    tok_rows, model_width = tokens.shape
    top_count = expert_ids.shape[1]
    experts = owner_map.shape[0]
    mean_load = tok_rows * top_count // experts
    capacity = mean_load + mean_load // 2
    normed = normalised(tokens, norm_gain)
    weights = gate_weights / jnp.sum(gate_weights, axis=1, keepdims=True)
    labels = jnp.arange(experts, dtype=jnp.int32)
    slot_table = jnp.sum(jnp.where(expert_ids[:, :, None] == labels, owner_map, 0), axis=2)
    flat_slot = slot_table.reshape(-1)
    onehot = (flat_slot[:, None] == labels).astype(jnp.bfloat16)
    count = flat_slot.shape[0]
    before = jnp.tri(count, count, -1, dtype=jnp.bfloat16)
    ranks = jnp.dot(before, onehot, preferred_element_type=jnp.float32)
    slot_rank = jnp.sum(ranks * onehot, axis=1).astype(jnp.int32)
    repeated = jnp.repeat(normed, top_count, axis=0)
    outgoing = (
        jnp.zeros((experts, capacity, model_width), jnp.bfloat16)
        .at[flat_slot, slot_rank]
        .set(repeated)
    )
    received = lax.all_to_all(outgoing, "tok", split_axis=0, concat_axis=0, tiled=True)
    source_count, slot_count, unused_width = received.shape
    flat_rows = received.reshape(source_count * slot_count, model_width)
    served = expert_rows(flat_rows, in_q[0], in_scale[0], down_q[0], down_scale[0])
    served = served.reshape(source_count, slot_count, model_width)
    returned_rows = lax.all_to_all(served, "tok", split_axis=0, concat_axis=0, tiled=True)
    picked = returned_rows[flat_slot, slot_rank].reshape(tok_rows, top_count, model_width)
    mixed = jnp.sum(weights[:, :, None] * picked.astype(jnp.float32), axis=1)
    return mixed.astype(jnp.bfloat16)


def ring_kernel(
    chips, experts, x_ref, in_hbm, in_scale_ref, down_hbm, down_scale_ref, out_ref,
    in_ref, down_ref, load_sem, rows, part, sib_in, ring_out, ring_in,
    right_send, right_recv, left_send, left_recv, sib_send, sib_recv,
    give_send, give_recv, sum_send, sum_recv,
):
    depth = chips // 2
    model = out_ref.shape[1]
    ways = ring_out.shape[0]
    wide = model // ways
    me = lax.axis_index("tok")
    core = lax.rem(me, 2)
    chip = me // 2
    place = chip // 2 + lax.rem(chip, 2) * (2 * depth - 1 - 2 * (chip // 2))

    def chip_at(position):
        position = lax.rem(position + 2 * chips, chips)
        back = position // depth
        return 2 * (position + back * (2 * depth - 1 - 2 * position)) + back

    right = 2 * chip_at(place + 1) + core
    left = 2 * chip_at(place - 1) + core
    sibling = 2 * chip + 1 - core

    def remote(src, dst, send, recv, target):
        return pltpu.make_async_remote_copy(
            src_ref=src, dst_ref=dst, send_sem=send, recv_sem=recv,
            device_id={"tok": target}, device_id_type=pl.DeviceIdType.MESH,
        )

    def row_copy(position, side, send, recv, target):
        block = rows.at[chip_at(position), side]
        return remote(block, block, send, recv, target)

    def go_right(k, position):
        return row_copy(position, core, right_send.at[k], right_recv.at[k], right)

    def go_left(k, position):
        return row_copy(position, core, left_send.at[k], left_recv.at[k], left)

    def share(offset, side):
        return row_copy(place + offset, side, sib_send.at[offset], sib_recv.at[offset], sibling)

    def give(offset):
        block = chip_at(place + offset)
        return remote(
            part.at[block, 1 - core], sib_in.at[block], give_send.at[offset], give_recv.at[offset], sibling
        )

    loads = (
        pltpu.make_async_copy(in_hbm, in_ref, load_sem.at[0]),
        pltpu.make_async_copy(down_hbm, down_ref, load_sem.at[1]),
    )
    for load in loads:
        load.start()
    rows[chip, core] = x_ref[...]
    barrier = pltpu.get_barrier_semaphore()
    for target in (left, right, sibling):
        pl.semaphore_signal(
            barrier, inc=1, device_id={"tok": target}, device_id_type=pl.DeviceIdType.MESH
        )
    pl.semaphore_wait(barrier, 3)

    far_right, far_left = chips // 2, chips - 1 - chips // 2
    go_right(0, place).start()
    go_left(0, place).start()
    share(0, core).start()
    for load in loads:
        load.wait()

    def sum_copy(way, step):
        target = right if way % 2 == 0 else left
        return remote(
            ring_out.at[way, step], ring_in.at[way, step],
            sum_send.at[way, step], sum_recv.at[way, step], target,
        )

    def own(offset, way):
        block = chip_at(place + offset)
        cut = slice(way * wide, (way + 1) * wide)
        return part[block, core, :, cut].astype(jnp.float32) + sib_in[block, :, cut].astype(jnp.float32)

    def sum_step(step, carry):
        for way in range(ways):
            offset = chips - 1 - step if way % 2 == 0 else 1 + step
            if way < 2:
                @pl.when((step < far_left) | ((step == far_left) & (way == 0)))
                def _():
                    give(offset).wait()

            mine = own(offset, way)
            sum_copy(way, step - 1).wait_recv()
            ring_out[way, step] = (mine + ring_in[way, step - 1].astype(jnp.float32)).astype(jnp.bfloat16)
            sum_copy(way, step).start()
        return carry

    def gather_step(k, carry):
        back = lax.rem(chips - k, chips)

        @pl.when(k >= 1)
        def _():
            go_right(k - 1, place - k).wait_recv()

            @pl.when(k < far_right)
            def _():
                go_right(k, place - k).start()

            share(back, core).start()

        @pl.when((k >= 1) & (k <= far_left))
        def _():
            go_left(k - 1, place + k).wait_recv()

            @pl.when(k < far_left)
            def _():
                go_left(k, place + k).start()

            share(k, core).start()

        sides = jnp.where((k >= 1) & (k <= far_left), 2, 1)

        def serve(turn, inner):
            offset = jnp.where(turn == 0, back, k)
            share(offset, 1 - core).wait_recv()
            block = chip_at(place + offset)
            batch = rows[block].reshape(-1, rows.shape[3])
            lanes = batch[:, model:].astype(jnp.float32)
            lane = lax.broadcasted_iota(jnp.int32, lanes.shape, 1)
            chosen = (lane == me) | (lane == me + experts) | (lane == me + 2 * experts)
            weight = jnp.sum(jnp.where(chosen, lanes, 0.0), axis=1, keepdims=True)
            values = batch[:, :model]
            gate = jnp.dot(values, in_ref[0], preferred_element_type=jnp.float32)
            gate = gate * in_scale_ref[0:1, :].astype(jnp.float32)
            up = jnp.dot(values, in_ref[1], preferred_element_type=jnp.float32)
            up = up * in_scale_ref[1:2, :].astype(jnp.float32)
            hidden = (gate / (1.0 + jnp.exp(-gate)) * up).astype(jnp.bfloat16)
            run = model // 4
            for piece in range(4):
                cut = slice(piece * run, (piece + 1) * run)
                served = jnp.dot(hidden, down_ref[:, cut], preferred_element_type=jnp.float32)
                served = served * down_scale_ref[:, cut].astype(jnp.float32) * weight
                part[block, :, :, cut] = served.astype(jnp.bfloat16).reshape(2, -1, run)
            give(offset).start()
            return inner

        lax.fori_loop(0, sides, serve, 0)

        @pl.when(k == 1)
        def _():
            give(chips - 1).wait()
            give(1).wait()
            for way in range(ways):
                first = chips - 1 if way % 2 == 0 else 1
                ring_out[way, 0] = own(first, way).astype(jnp.bfloat16)
                sum_copy(way, 0).start()

        @pl.when(k >= 2)
        def _():
            sum_step(k - 1, 0)

        return carry

    lax.fori_loop(0, far_right + 1, gather_step, 0)

    lax.fori_loop(far_right, chips - 1, sum_step, 0)
    give(0).wait()
    for way in range(ways):
        mine = own(0, way)
        sum_copy(way, chips - 2).wait_recv()
        total = mine + ring_in[way, chips - 2].astype(jnp.float32)
        out_ref[:, way * wide : (way + 1) * wide] = total.astype(jnp.bfloat16)

    def ended(step, carry):
        for way in range(ways):
            sum_copy(way, step).wait_send()
        return carry

    lax.fori_loop(0, chips - 1, ended, 0)

    def shared(offset, carry):
        share(offset, core).wait_send()
        return carry

    lax.fori_loop(0, chips, shared, 0)
    for k in range(far_right):
        go_right(k, place - k).wait_send()
    for k in range(far_left):
        go_left(k, place + k).wait_send()


def gathered(
    tokens, norm_gain, expert_ids, gate_weights, owner_map, in_q, in_scale, down_q, down_scale
):
    experts = owner_map.shape[0]
    tok_rows, model = tokens.shape
    chips = experts // 2
    normed = normalised(tokens, norm_gain)
    weights = gate_weights / jnp.sum(gate_weights, axis=1, keepdims=True)
    labels = jnp.arange(experts, dtype=jnp.int32)
    slot_table = jnp.sum(jnp.where(expert_ids[:, :, None] == labels, owner_map, 0), axis=2)
    shares = jnp.sum(jnp.where(slot_table[:, :, None] == labels, weights[:, :, None], 0.0), axis=1)
    high = lax.reduce_precision(shares, 8, 7)
    middle = lax.reduce_precision(shares - high, 8, 7)
    low = shares - high - middle
    lanes = jnp.concatenate([high, middle, low], axis=1).astype(jnp.bfloat16)
    pad = -lanes.shape[1] % 128
    rows = jnp.concatenate([normed, jnp.pad(lanes, ((0, 0), (0, pad)))], axis=1)
    width = rows.shape[1]
    vmem = pl.BlockSpec(memory_space=pltpu.VMEM)
    dma = pltpu.SemaphoreType.DMA
    total_rows = 2 * chips * tok_rows
    ways = 4
    return pl.pallas_call(
        functools.partial(ring_kernel, chips, experts),
        out_shape=jax.ShapeDtypeStruct((tok_rows, model), jnp.bfloat16),
        in_specs=[vmem, pl.BlockSpec(memory_space=pl.ANY), vmem, pl.BlockSpec(memory_space=pl.ANY), vmem],
        out_specs=vmem,
        scratch_shapes=[
            pltpu.VMEM(in_q.shape[1:], in_q.dtype),
            pltpu.VMEM(down_q.shape[1:], down_q.dtype),
            dma((2,)),
            pltpu.VMEM((chips, 2, tok_rows, width), jnp.bfloat16),
            pltpu.VMEM((chips, 2, tok_rows, model), jnp.bfloat16),
            pltpu.VMEM((chips, tok_rows, model), jnp.bfloat16),
            pltpu.VMEM((ways, chips - 1, tok_rows, model // ways), jnp.bfloat16),
            pltpu.VMEM((ways, chips - 1, tok_rows, model // ways), jnp.bfloat16),
            dma((chips,)), dma((chips,)), dma((chips,)), dma((chips,)), dma((chips,)), dma((chips,)),
            dma((chips,)), dma((chips,)), dma((ways, chips - 1)), dma((ways, chips - 1)),
        ],
        compiler_params=pltpu.CompilerParams(
            collective_id=0, has_side_effects=True, vmem_limit_bytes=60 * 1024 * 1024
        ),
        cost_estimate=pl.CostEstimate(
            flops=6 * total_rows * model * in_q.shape[3], bytes_accessed=4 * total_rows * model, transcendentals=0
        ),
    )(rows, in_q[0], in_scale[0], down_q[0], down_scale)


def solution(mesh):
    in_specs = (
        P(("grp", "tok"), None),
        P(),
        P(("grp", "tok"), None),
        P(("grp", "tok"), None),
        P(),
        P("tok", None, None, None),
        P("tok", None, None),
        P("tok", None, None),
        P("tok", None),
    )
    out_specs = P(("grp", "tok"), None)

    def on_device(*args):
        experts, top_count = args[4].shape[0], args[2].shape[1]
        body = gathered if experts <= 2 * top_count and experts % 4 == 0 else dispatched
        return body(*args)

    return jax.shard_map(
        on_device, mesh=mesh, in_specs=in_specs, out_specs=out_specs, check_vma=False
    )
```

```python
import functools

import jax
import jax.numpy as jnp
from jax import lax
from jax.experimental import pallas as pl
from jax.experimental.pallas import tpu as pltpu
from jax.sharding import PartitionSpec as P


def expert_rows(batch_rows, in_blocks, in_scales, down_block, down_scales):
    gate_part = jnp.dot(batch_rows, in_blocks[0], preferred_element_type=jnp.float32) * in_scales[0]
    up_part = jnp.dot(batch_rows, in_blocks[1], preferred_element_type=jnp.float32) * in_scales[1]
    hidden = (jax.nn.silu(gate_part) * up_part).astype(jnp.bfloat16)
    return (jnp.dot(hidden, down_block, preferred_element_type=jnp.float32) * down_scales).astype(
        jnp.bfloat16
    )


def normalised(tokens, norm_gain):
    values = tokens.astype(jnp.float32)
    row_scale = lax.rsqrt(jnp.mean(values * values, axis=1, keepdims=True) + 1e-06)
    return (values * row_scale * norm_gain).astype(jnp.bfloat16)


def dispatched(
    tokens, norm_gain, expert_ids, gate_weights, owner_map, in_q, in_scale, down_q, down_scale
):
    tok_rows, model_width = tokens.shape
    top_count = expert_ids.shape[1]
    experts = owner_map.shape[0]
    mean_load = tok_rows * top_count // experts
    capacity = mean_load + mean_load // 2
    normed = normalised(tokens, norm_gain)
    weights = gate_weights / jnp.sum(gate_weights, axis=1, keepdims=True)
    labels = jnp.arange(experts, dtype=jnp.int32)
    slot_table = jnp.sum(jnp.where(expert_ids[:, :, None] == labels, owner_map, 0), axis=2)
    flat_slot = slot_table.reshape(-1)
    onehot = (flat_slot[:, None] == labels).astype(jnp.bfloat16)
    count = flat_slot.shape[0]
    before = jnp.tri(count, count, -1, dtype=jnp.bfloat16)
    ranks = jnp.dot(before, onehot, preferred_element_type=jnp.float32)
    slot_rank = jnp.sum(ranks * onehot, axis=1).astype(jnp.int32)
    repeated = jnp.repeat(normed, top_count, axis=0)
    outgoing = (
        jnp.zeros((experts, capacity, model_width), jnp.bfloat16)
        .at[flat_slot, slot_rank]
        .set(repeated)
    )
    received = lax.all_to_all(outgoing, "tok", split_axis=0, concat_axis=0, tiled=True)
    source_count, slot_count, unused_width = received.shape
    flat_rows = received.reshape(source_count * slot_count, model_width)
    served = expert_rows(flat_rows, in_q[0], in_scale[0], down_q[0], down_scale[0])
    served = served.reshape(source_count, slot_count, model_width)
    returned_rows = lax.all_to_all(served, "tok", split_axis=0, concat_axis=0, tiled=True)
    picked = returned_rows[flat_slot, slot_rank].reshape(tok_rows, top_count, model_width)
    mixed = jnp.sum(weights[:, :, None] * picked.astype(jnp.float32), axis=1)
    return mixed.astype(jnp.bfloat16)


def ring_kernel(
    chips, experts, x_ref, gain_ref, ids_ref, gates_ref, owner_ref, in_hbm, in_scale_ref, down_hbm, down_scale_ref, out_ref,
    in_ref, down_ref, load_sem, rows, part, sib_in, ring_out, ring_in,
    right_send, right_recv, left_send, left_recv, sib_send, sib_recv,
    give_send, give_recv, sum_send, sum_recv,
):
    depth = chips // 2
    model = out_ref.shape[1]
    ways = ring_out.shape[0]
    wide = model // ways
    me = lax.axis_index("tok")
    core = lax.rem(me, 2)
    chip = me // 2
    place = chip // 2 + lax.rem(chip, 2) * (2 * depth - 1 - 2 * (chip // 2))

    def chip_at(position):
        position = lax.rem(position + 2 * chips, chips)
        back = position // depth
        return 2 * (position + back * (2 * depth - 1 - 2 * position)) + back

    right = 2 * chip_at(place + 1) + core
    left = 2 * chip_at(place - 1) + core
    sibling = 2 * chip + 1 - core

    def remote(src, dst, send, recv, target):
        return pltpu.make_async_remote_copy(
            src_ref=src, dst_ref=dst, send_sem=send, recv_sem=recv,
            device_id={"tok": target}, device_id_type=pl.DeviceIdType.MESH,
        )

    def row_copy(position, side, send, recv, target):
        block = rows.at[chip_at(position), side]
        return remote(block, block, send, recv, target)

    def go_right(k, position):
        return row_copy(position, core, right_send.at[k], right_recv.at[k], right)

    def go_left(k, position):
        return row_copy(position, core, left_send.at[k], left_recv.at[k], left)

    far_right, far_left = chips // 2, chips - 1 - chips // 2
    tok_half = x_ref.shape[0] // 2

    def far_rows(position, low):
        return rows.at[chip_at(position), core, low * tok_half : (low + 1) * tok_half]

    def end_right(position):
        block = far_rows(position, 0)
        return remote(block, block, right_send.at[far_right - 1], right_recv.at[far_right - 1], right)

    def end_left(position):
        block = far_rows(position, 1)
        return remote(block, block, left_send.at[far_left], left_recv.at[far_left], left)

    def share(offset, side):
        return row_copy(place + offset, side, sib_send.at[offset], sib_recv.at[offset], sibling)

    def give(offset):
        block = chip_at(place + offset)
        return remote(
            part.at[block, 1 - core], sib_in.at[block], give_send.at[offset], give_recv.at[offset], sibling
        )

    loads = (
        pltpu.make_async_copy(in_hbm, in_ref, load_sem.at[0]),
        pltpu.make_async_copy(down_hbm, down_ref, load_sem.at[1]),
    )
    for load in loads:
        load.start()
    barrier = pltpu.get_barrier_semaphore()
    for target in (left, right, sibling):
        pl.semaphore_signal(
            barrier, inc=1, device_id={"tok": target}, device_id_type=pl.DeviceIdType.MESH
        )

    values = x_ref[...].astype(jnp.float32)
    row_scale = lax.rsqrt(jnp.mean(values * values, axis=1, keepdims=True) + 1e-06)
    rows[chip, core, :, :model] = (values * row_scale * gain_ref[...]).astype(jnp.bfloat16)
    weights = gates_ref[...] / jnp.sum(gates_ref[...], axis=1, keepdims=True)
    lane = lax.broadcasted_iota(jnp.int32, (x_ref.shape[0], rows.shape[3] - model), 1)
    named = jnp.full(lane.shape, -1, jnp.int32)
    for expert in range(experts):
        slot = owner_ref[expert]
        served_there = (lane == slot) | (lane == slot + experts) | (lane == slot + 2 * experts)
        named = jnp.where(served_there, expert, named)
    shares = jnp.zeros(lane.shape, jnp.float32)
    for k in range(ids_ref.shape[1]):
        shares += jnp.where(ids_ref[:, k : k + 1] == named, weights[:, k : k + 1], 0.0)
    high = shares.astype(jnp.bfloat16).astype(jnp.float32)
    middle = (shares - high).astype(jnp.bfloat16).astype(jnp.float32)
    low = shares - high - middle
    split = jnp.where(lane < experts, high, jnp.where(lane < 2 * experts, middle, low))
    rows[chip, core, :, model:] = split.astype(jnp.bfloat16)
    pl.semaphore_wait(barrier, 3)

    go_right(0, place).start()
    go_left(0, place).start()
    share(0, core).start()
    for load in loads:
        load.wait()

    def sum_copy(way, step):
        target = right if way % 2 == 0 else left
        return remote(
            ring_out.at[way, step], ring_in.at[way, step],
            sum_send.at[way, step], sum_recv.at[way, step], target,
        )

    def own(offset, way):
        block = chip_at(place + offset)
        cut = slice(way * wide, (way + 1) * wide)
        return part[block, core, :, cut].astype(jnp.float32) + sib_in[block, :, cut].astype(jnp.float32)

    def sum_step(step, carry):
        for way in range(ways):
            offset = chips - 1 - step if way % 2 == 0 else 1 + step
            if way < 2:
                @pl.when((step < far_left) | ((step == far_left) & (way == 0)))
                def _():
                    give(offset).wait()

            mine = own(offset, way)
            sum_copy(way, step - 1).wait_recv()
            ring_out[way, step] = (mine + ring_in[way, step - 1].astype(jnp.float32)).astype(jnp.bfloat16)
            sum_copy(way, step).start()
        return carry

    def gather_step(k, carry):
        back = lax.rem(chips - k, chips)

        @pl.when((k >= 1) & (k <= far_left))
        def _():
            go_right(k - 1, place - k).wait_recv()

            @pl.when(k < far_left)
            def _():
                go_right(k, place - k).start()

            @pl.when(k == far_left)
            def _():
                end_right(place - k).start()

            share(back, core).start()
            go_left(k - 1, place + k).wait_recv()

            @pl.when(k < far_left)
            def _():
                go_left(k, place + k).start()

            @pl.when(k == far_left)
            def _():
                end_left(place + k).start()

            share(k, core).start()

        @pl.when(k == far_right)
        def _():
            end_right(place - k).wait_recv()
            end_left(place + k).wait_recv()
            share(back, core).start()

        sides = jnp.where((k >= 1) & (k <= far_left), 2, 1)

        def serve(turn, inner):
            offset = jnp.where(turn == 0, back, k)
            share(offset, 1 - core).wait_recv()
            block = chip_at(place + offset)
            batch = rows[block].reshape(-1, rows.shape[3])
            lanes = batch[:, model:].astype(jnp.float32)
            lane = lax.broadcasted_iota(jnp.int32, lanes.shape, 1)
            chosen = (lane == me) | (lane == me + experts) | (lane == me + 2 * experts)
            weight = jnp.sum(jnp.where(chosen, lanes, 0.0), axis=1, keepdims=True)
            values = batch[:, :model]
            gate = jnp.dot(values, in_ref[0], preferred_element_type=jnp.float32)
            gate = gate * in_scale_ref[0:1, :].astype(jnp.float32)
            up = jnp.dot(values, in_ref[1], preferred_element_type=jnp.float32)
            up = up * in_scale_ref[1:2, :].astype(jnp.float32)
            hidden = (gate / (1.0 + jnp.exp(-gate)) * up).astype(jnp.bfloat16)
            run = model // 4
            for piece in range(4):
                cut = slice(piece * run, (piece + 1) * run)
                served = jnp.dot(hidden, down_ref[:, cut], preferred_element_type=jnp.float32)
                served = served * down_scale_ref[:, cut].astype(jnp.float32) * weight
                part[block, :, :, cut] = served.astype(jnp.bfloat16).reshape(2, -1, run)
            give(offset).start()
            return inner

        lax.fori_loop(0, sides, serve, 0)

        @pl.when(k == 1)
        def _():
            give(chips - 1).wait()
            give(1).wait()
            for way in range(ways):
                first = chips - 1 if way % 2 == 0 else 1
                ring_out[way, 0] = own(first, way).astype(jnp.bfloat16)
                sum_copy(way, 0).start()

        @pl.when(k >= 2)
        def _():
            sum_step(k - 1, 0)

        return carry

    lax.fori_loop(0, far_right + 1, gather_step, 0)

    lax.fori_loop(far_right, chips - 1, sum_step, 0)
    give(0).wait()
    for way in range(ways):
        mine = own(0, way)
        sum_copy(way, chips - 2).wait_recv()
        total = mine + ring_in[way, chips - 2].astype(jnp.float32)
        out_ref[:, way * wide : (way + 1) * wide] = total.astype(jnp.bfloat16)

    def ended(step, carry):
        for way in range(ways):
            sum_copy(way, step).wait_send()
        return carry

    lax.fori_loop(0, chips - 1, ended, 0)

    def shared(offset, carry):
        share(offset, core).wait_send()
        return carry

    lax.fori_loop(0, chips, shared, 0)
    for k in range(far_left):
        go_right(k, place - k).wait_send()
        go_left(k, place + k).wait_send()
    end_right(place - far_left).wait_send()
    end_left(place + far_left).wait_send()


def gathered(
    tokens, norm_gain, expert_ids, gate_weights, owner_map, in_q, in_scale, down_q, down_scale
):
    experts = owner_map.shape[0]
    tok_rows, model = tokens.shape
    chips = experts // 2
    width = model + 128 * ((3 * experts + 127) // 128)
    vmem = pl.BlockSpec(memory_space=pltpu.VMEM)
    dma = pltpu.SemaphoreType.DMA
    total_rows = 2 * chips * tok_rows
    ways = 4
    return pl.pallas_call(
        functools.partial(ring_kernel, chips, experts),
        out_shape=jax.ShapeDtypeStruct((tok_rows, model), jnp.bfloat16),
        in_specs=[vmem] * 4 + [pl.BlockSpec(memory_space=pltpu.SMEM), pl.BlockSpec(memory_space=pl.ANY), vmem, pl.BlockSpec(memory_space=pl.ANY), vmem],
        out_specs=vmem,
        scratch_shapes=[
            pltpu.VMEM(in_q.shape[1:], in_q.dtype),
            pltpu.VMEM(down_q.shape[1:], down_q.dtype),
            dma((2,)),
            pltpu.VMEM((chips, 2, tok_rows, width), jnp.bfloat16),
            pltpu.VMEM((chips, 2, tok_rows, model), jnp.bfloat16),
            pltpu.VMEM((chips, tok_rows, model), jnp.bfloat16),
            pltpu.VMEM((ways, chips - 1, tok_rows, model // ways), jnp.bfloat16),
            pltpu.VMEM((ways, chips - 1, tok_rows, model // ways), jnp.bfloat16),
            dma((chips,)), dma((chips,)), dma((chips,)), dma((chips,)), dma((chips,)), dma((chips,)),
            dma((chips,)), dma((chips,)), dma((ways, chips - 1)), dma((ways, chips - 1)),
        ],
        compiler_params=pltpu.CompilerParams(
            collective_id=0, has_side_effects=True, vmem_limit_bytes=60 * 1024 * 1024
        ),
        cost_estimate=pl.CostEstimate(
            flops=6 * total_rows * model * in_q.shape[3], bytes_accessed=4 * total_rows * model, transcendentals=0
        ),
    )(tokens, norm_gain[None, :], expert_ids, gate_weights, owner_map, in_q[0], in_scale[0], down_q[0], down_scale)


def solution(mesh):
    in_specs = (
        P(("grp", "tok"), None),
        P(),
        P(("grp", "tok"), None),
        P(("grp", "tok"), None),
        P(),
        P("tok", None, None, None),
        P("tok", None, None),
        P("tok", None, None),
        P("tok", None),
    )
    out_specs = P(("grp", "tok"), None)

    def on_device(*args):
        experts, top_count = args[4].shape[0], args[2].shape[1]
        body = gathered if experts <= 2 * top_count and experts % 8 == 0 else dispatched
        return body(*args)

    return jax.shard_map(
        on_device, mesh=mesh, in_specs=in_specs, out_specs=out_specs, check_vma=False
    )
```
